256 devices in a mesh: fsdp: 8 (over z), tp: 8 (over x, core), rep: 4 (over y).
Axes of the slice: x: 4, y: 4, z: 8, core: 2. Of those that a mesh axis runs over, the one named last changes fastest.
Arguments:
- weight: float32 [4096, 16384], P('fsdp', 'tp'), may hold values from -6 to 6
- momentum: float32 [4, 4096, 16384], P('rep', 'fsdp', 'tp'), may hold values from -24 to 24
- gradient: bfloat16 [4, 4096, 16384], P('rep', 'fsdp', 'tp'), may hold values from -6 to 6
- q_in: float32 [16384, 128], P('tp'), may hold values from -6 to 6
Outputs:
- weight_new: float32 [4096, 16384], P('fsdp', 'tp')
- momentum_new: float32 [4, 4096, 16384], P('rep', 'fsdp', 'tp')
- q_new: float32 [16384, 128], P('tp')
The draws below stay inside these ranges and needn't reach their ends.
All inputs are finite; a program needn't handle non-finite values.
Results may differ from the reference program's by a relative error of at most 0.0003.
Values sent between devices are 32-bit elements; how exact they have to be, the bound alone decides.
A program may use at most 64 MiB of HBM per device.

```python
import jax
import jax.numpy as jnp
from jax import lax

N = 16384
RANK = 128
M = 4096
REPLICAS = 4


def draw_momentum(key, part):
    key = jax.random.fold_in(key, 7)
    left_key, right_key, noise_key = jax.random.split(key, 3)
    left_factors = jnp.clip(jax.random.normal(left_key, (8, M, 1), jnp.float32), -4.0, 4.0)
    right_factors = jnp.clip(jax.random.normal(right_key, (8, 1, N), jnp.float32), -4.0, 4.0)
    noise = jnp.clip(jax.random.normal(noise_key, (REPLICAS, M, N), jnp.float32), -6.0, 6.0)
    shared = jnp.zeros((M, N), jnp.float32)
    for term in range(8):
        shared = shared + left_factors[term] * right_factors[term]
    return jnp.clip(1.1 * shared[None] + noise, -24.0, 24.0)


def shard_levels(stream_key, extent, cuts, least, high):
    level, own = 1.0, jax.random.fold_in(stream_key, 6)
    for position, parts in cuts:
        heights = jnp.exp(jax.random.uniform(jax.random.fold_in(own, position), (parts,), jnp.float32, least / len(cuts), high / len(cuts)))
        level = level * jnp.repeat(heights, extent[position] // parts).reshape([-1 if axis == position else 1 for axis in range(len(extent))])
    return level


def centred(stream_key, extent, deviation, most, pieces=(), kind=jnp.bfloat16):
    array = jax.random.normal(stream_key, extent, jnp.float32) * deviation
    if len(pieces) > 0:
        array = shard_levels(stream_key, extent, pieces, -0.22, 0.18) * array
    return jnp.clip(array, min=-most, max=most).astype(kind)


def setup_inputs(seed: int = 0) -> dict:
    splits = jax.random.split(jax.random.key(seed), 5)
    return {
        "weight": centred(splits[0], (M, N), 1.0, 6.0, ((0, 8), (1, 8)), jnp.float32),
        "momentum": draw_momentum(jax.random.fold_in(splits[4], 71), 0),
        "gradient": centred(splits[2], (REPLICAS, M, N), 1.0, 6.0, ((0, 4), (1, 8), (2, 8))),
        "q_in": centred(splits[3], (N, RANK), 1.0, 6.0, ((0, 8),), jnp.float32),
    }


def reference(weight, momentum, gradient, q_in):
    high = lax.Precision.HIGHEST
    projected = jnp.zeros((M, RANK), jnp.float32)
    for index in range(REPLICAS):
        buffer = momentum[index] + gradient[index].astype(jnp.float32)
        projected = projected + jnp.dot(buffer.astype(jnp.float32), q_in.astype(jnp.float32), precision=high, preferred_element_type=jnp.float32)
    projected = projected / REPLICAS
    gram = jnp.dot(projected.T.astype(jnp.float32), projected.astype(jnp.float32), precision=high, preferred_element_type=jnp.float32)
    lower = jnp.linalg.cholesky(gram)
    basis = jax.scipy.linalg.solve_triangular(lower, projected.T, lower=True).T
    right = jnp.zeros((N, RANK), jnp.float32)
    for index in range(REPLICAS):
        buffer = momentum[index] + gradient[index].astype(jnp.float32)
        right = right + jnp.dot(buffer.T.astype(jnp.float32), basis.astype(jnp.float32), precision=high, preferred_element_type=jnp.float32)
    right = right / REPLICAS
    q_new = right * lax.rsqrt(lax.optimization_barrier(jnp.sum(right * right, axis=0)) / N + 1e-06)
    feedback = jnp.dot(basis.astype(jnp.float32), right.T.astype(jnp.float32), precision=high, preferred_element_type=jnp.float32)
    momentum_new = jnp.stack([momentum[index] + gradient[index].astype(jnp.float32) - 0.05 * feedback for index in range(REPLICAS)])
    weight_new = 0.999 * weight - 0.2 * jnp.dot(basis.astype(jnp.float32), q_new.T.astype(jnp.float32), precision=high, preferred_element_type=jnp.float32)
    return (weight_new, momentum_new, q_new)
```

```python
import jax
import jax.numpy as jnp
from jax import lax
from jax.experimental import pallas as pl
from jax.experimental.pallas import tpu as pltpu
from jax.sharding import PartitionSpec as P

MESH = pl.DeviceIdType.MESH
F32 = jnp.float32
BF16 = jnp.bfloat16
Z, T, Y = 8, 8, 4
G = T * Y


def split(x):
    hi = x.astype(BF16)
    return hi, (x - hi.astype(F32)).astype(BF16)


def mm(a, b, dims=((1,), (0,))):
    return lax.dot_general(a, b, (dims, ((), ())), preferred_element_type=F32)


def mmf(a, b, dims=((1,), (0,))):
    return lax.dot_general(a, b, (dims, ((), ())), precision=lax.Precision.HIGHEST, preferred_element_type=F32)


class Exchange:
    def __init__(self, n, me, device, src, dst, send, recv):
        self.n, self.me, self.device, self.src, self.dst = n, me, device, src, dst
        self.send, self.recv = send, recv

    def each(self, body):
        def step(o, carry):
            body(lax.rem(self.me + o, self.n))
            return carry

        lax.fori_loop(1, self.n, step, 0)

    def copy(self, j, slot):
        return pltpu.make_async_remote_copy(
            src_ref=self.src(j),
            dst_ref=self.dst(slot),
            send_sem=self.send.at[j],
            recv_sem=self.recv.at[slot],
            device_id=self.device(j),
            device_id_type=MESH,
        )

    def start(self):
        self.each(lambda j: self.copy(j, self.me).start())

    def wait_recv(self):
        self.each(lambda j: self.copy(j, j).wait_recv())

    def wait_send(self):
        self.each(lambda j: self.copy(j, self.me).wait_send())


def total(ref, n):
    acc = ref[0]
    for k in range(1, n):
        acc = acc + ref[k]
    return acc


def factor(work, gram):
    rows = lax.broadcasted_iota(jnp.int32, (128, 128), 0)
    lanes = lax.broadcasted_iota(jnp.int32, (128, 128), 1)
    work[:, 0:128] = gram
    work[:, 128:256] = jnp.where(rows == lanes, 1.0, 0.0).astype(F32)

    def pivot(j, carry):
        row = work[pl.ds(j, 1), :]
        left = work[:, 0:128]
        col = jnp.sum(jnp.where(lanes == j, left, 0.0), axis=1, keepdims=True)
        d = jnp.sum(jnp.where(lanes[0:1] == j, row[:, 0:128], 0.0), axis=1, keepdims=True)
        m = jnp.where(rows[:, 0:1] > j, col * (1.0 / d), 0.0)
        work[...] = work[...] - m * row
        return carry

    lax.fori_loop(0, 128, pivot, 0)
    d = jnp.sum(jnp.where(rows == lanes, work[:, 0:128], 0.0), axis=1, keepdims=True)
    return work[:, 128:256] * lax.rsqrt(d)


def talk(
    mom, grad, q_in, right_out, basis_out, sq_out,
    mom_v, grad_v, q_v, hi_v, lo_v, q_hl,
    part, part_r, proj, gram_p, gram_r, gram,
    wa, wb, ra1, rb1, sa1, sb1, ra2, rb2, rta, rtb,
    work, basis_v, sq_t, sq_y, sq_z,
    load, store, s_tp, r_tp, s_z, r_z, s_y, r_y,
):
    f, t, r = lax.axis_index("fsdp"), lax.axis_index("tp"), lax.axis_index("rep")
    g = t * Y + r

    loads = [pltpu.make_async_copy(q_in, q_v, load.at[8])]
    for c in range(4):
        cols = pl.ds(512 * c, 512)
        loads.append(pltpu.make_async_copy(mom.at[:, cols], mom_v.at[:, cols], load.at[2 * c]))
        loads.append(pltpu.make_async_copy(grad.at[:, cols], grad_v.at[:, cols], load.at[2 * c + 1]))
    for cp in loads:
        cp.start()

    plane = lambda j: {"tp": lax.div(j, Y), "rep": lax.rem(j, Y)}
    along_z = lambda j: {"fsdp": j}
    along_y = lambda j: {"rep": j}
    along_t = lambda j: {"tp": j}

    barrier = pltpu.get_barrier_semaphore()

    def greet(n, me, device):
        def step(o, carry):
            pl.semaphore_signal(barrier, inc=1, device_id=device(lax.rem(me + o, n)), device_id_type=MESH)
            return carry

        lax.fori_loop(1, n, step, 0)

    greet(G, g, plane)
    greet(Z, f, along_z)

    ex_part = Exchange(G, g, plane, lambda j: part.at[j], lambda i: part_r.at[i], s_tp.at[0], r_tp.at[0])
    ex_proj = Exchange(G, g, plane, lambda j: proj.at[g], lambda i: proj.at[i], s_tp.at[1], r_tp.at[1])
    ex_gram = Exchange(Z, f, along_z, lambda j: gram_p.at[j], lambda i: gram_r.at[i], s_z.at[0], r_z.at[0])
    ex_gall = Exchange(Z, f, along_z, lambda j: gram.at[f], lambda i: gram.at[i], s_z.at[1], r_z.at[1])
    ex_a1 = Exchange(Z, f, along_z, lambda j: wa.at[j], lambda i: ra1.at[i], s_z.at[2], r_z.at[2])
    ex_b1 = Exchange(Y, r, along_y, lambda j: wb.at[j], lambda i: rb1.at[i], s_y.at[0], r_y.at[0])
    ex_a2 = Exchange(Y, r, along_y, lambda j: sa1.at[j], lambda i: ra2.at[i], s_y.at[1], r_y.at[1])
    ex_b2 = Exchange(Z, f, along_z, lambda j: sb1.at[j], lambda i: rb2.at[i], s_z.at[3], r_z.at[3])
    ga1 = Exchange(Y, r, along_y, lambda j: rta.at[f, r], lambda i: rta.at[f, i], s_y.at[2], r_y.at[2])
    gb1 = Exchange(Z, f, along_z, lambda j: rtb.at[r, f], lambda i: rtb.at[r, i], s_z.at[4], r_z.at[4])
    ga2 = Exchange(Z, f, along_z, lambda j: rta.at[f], lambda i: rta.at[i], s_z.at[5], r_z.at[5])
    gb2 = Exchange(Y, r, along_y, lambda j: rtb.at[r], lambda i: rtb.at[i], s_y.at[3], r_y.at[3])
    ex_qt = Exchange(T, t, along_t, lambda j: sq_t.at[t], lambda i: sq_t.at[i], s_z.at[6], r_z.at[6])
    ex_qy = Exchange(Y, r, along_y, lambda j: sq_y.at[r], lambda i: sq_y.at[i], s_y.at[4], r_y.at[4])
    ex_qz = Exchange(Z, f, along_z, lambda j: sq_z.at[f], lambda i: sq_z.at[i], s_z.at[7], r_z.at[7])

    loads[0].wait()
    q_h, q_l = split(q_v[...])
    q_hl[:, 0:128] = q_h
    q_hl[:, 128:256] = q_l
    acc = None
    for c in range(4):
        cols = pl.ds(512 * c, 512)
        loads[2 * c + 1].wait()
        loads[2 * c + 2].wait()
        b_h, b_l = split(mom_v[:, cols] + grad_v[:, cols].astype(F32))
        hi_v[:, cols] = b_h
        lo_v[:, cols] = b_l
        both = mm(b_h, q_hl[cols, :])
        term = both[:, 0:128] + (both[:, 128:256] + mm(b_l, q_hl[cols, 0:128]))
        acc = term if acc is None else acc + term
    part[...] = acc.reshape(G, 16, 128)
    part_r[pl.ds(g, 1)] = part[pl.ds(g, 1)]

    pl.semaphore_wait(barrier, G + Z - 2)
    ex_part.start()
    ex_part.wait_recv()
    proj[pl.ds(g, 1)] = total(part_r, G)[None]
    ex_proj.start()
    ex_proj.wait_recv()

    p = proj[...].reshape(512, 128)
    pt = p.T
    pt_h, pt_l = split(pt)
    gram_p[...] = mmf(pt, p).reshape(Z, 16, 128)
    gram_r[pl.ds(f, 1)] = gram_p[pl.ds(f, 1)]
    ex_gram.start()

    def columns(lo, n):
        b_h = hi_v[:, lo : lo + n]
        w = mm(pt_h, b_h) + (mm(pt_l, b_h) + mm(pt_h, lo_v[:, lo : lo + n]))
        return w.T

    for c in range(2):
        wa[4 * c : 4 * c + 4] = columns(512 * c, 512).reshape(4, 128, 128)
    ra1[pl.ds(f, 1)] = wa[pl.ds(f, 1)]
    ex_a1.start()
    for c in range(2):
        wb[2 * c : 2 * c + 2] = columns(1024 + 512 * c, 512).reshape(2, 256, 128)
    rb1[pl.ds(r, 1)] = wb[pl.ds(r, 1)]
    ex_b1.start()

    ex_gram.wait_recv()
    gram[pl.ds(f, 1)] = total(gram_r, Z)[None]
    ex_gall.start()

    ex_b1.wait_recv()
    sb1[...] = total(rb1, Y).reshape(Z, 32, 128)
    rb2[pl.ds(f, 1)] = sb1[pl.ds(f, 1)]
    ex_b2.start()
    ex_a1.wait_recv()
    sa1[...] = total(ra1, Z).reshape(Y, 32, 128)
    ra2[pl.ds(r, 1)] = sa1[pl.ds(r, 1)]
    ex_a2.start()

    ex_gall.wait_recv()
    inverse = factor(work, gram[...].reshape(128, 128))

    ex_a2.wait_recv()
    ex_b2.wait_recv()
    w = jnp.concatenate([total(ra2, Y), total(rb2, Z)], axis=0)
    right = 0.25 * mmf(w, inverse, ((1,), (1,)))
    rta[pl.ds(f, 1), pl.ds(r, 1)] = right[0:32][None, None]
    rtb[pl.ds(r, 1), pl.ds(f, 1)] = right[32:64][None, None]
    ga1.start()
    gb1.start()
    squares = jnp.sum(right * right, axis=0, keepdims=True)
    sq_t[pl.ds(t, 1)] = jnp.broadcast_to(squares, (8, 128))[None]
    ex_qt.start()
    basis_v[...] = mmf(p, inverse, ((1,), (1,)))
    keep_basis = pltpu.make_async_copy(basis_v, basis_out, store.at[0])
    keep_basis.start()

    ex_qt.wait_recv()
    sq_y[pl.ds(r, 1)] = total(sq_t, T)[None]
    ex_qy.start()
    ga1.wait_recv()
    ga2.start()
    ex_qy.wait_recv()
    sq_z[pl.ds(f, 1)] = total(sq_y, Y)[None]
    ex_qz.start()
    gb1.wait_recv()
    gb2.start()
    ex_qz.wait_recv()
    sq_out[...] = total(sq_z, Z)
    gb2.wait_recv()
    keep_b = pltpu.make_async_copy(rtb, right_out.at[1], store.at[1])
    keep_a = pltpu.make_async_copy(rta.reshape(Y, Z, 32, 128), right_out.at[0], store.at[2])
    keep_b.start()
    ga2.wait_recv()
    keep_a.start()
    for ex in (ex_part, ex_proj, ex_gram, ex_gall, ex_a1, ex_b1, ex_a2, ex_b2, ga1, gb1, ga2, gb2, ex_qt, ex_qy, ex_qz):
        ex.wait_send()
    keep_basis.wait()
    keep_b.wait()
    keep_a.wait()


def finish(mom, grad, weight, right, basis, sq, weight_out, mom_out, q_out):
    r = right[...]
    scale = lax.rsqrt(sq[0:1] * (1.0 / 16384.0) + 1e-06)
    q_out[...] = r * scale
    r_h, r_l = split(r)
    nt = ((1,), (1,))
    b = basis[...]
    b_h, b_l = split(b)
    feedback = mm(b_h, r_h, nt) + (mm(b_h, r_l, nt) + mm(b_l, r_h, nt))
    mom_out[...] = (mom[...] + grad[...].astype(F32)) - 0.05 * feedback
    s_h, s_l = split(b * scale)
    update = mm(s_h, r_h, nt) + (mm(s_h, r_l, nt) + mm(s_l, r_h, nt))
    weight_out[...] = 0.999 * weight[...] - 0.2 * update


def shards(weight, momentum, gradient, q_in):
    mom, grad = momentum[0], gradient[0]
    vm = lambda *shape: pltpu.VMEM(shape, F32)
    dma = lambda *shape: pltpu.SemaphoreType.DMA(shape)
    any_ = pl.BlockSpec(memory_space=pl.ANY)
    right, basis, sq = pl.pallas_call(
        talk,
        out_shape=(
            jax.ShapeDtypeStruct((2, Y, Z, 32, 128), F32),
            jax.ShapeDtypeStruct((512, 128), F32),
            jax.ShapeDtypeStruct((8, 128), F32),
        ),
        in_specs=[any_] * 3,
        out_specs=(any_, any_, pl.BlockSpec(memory_space=pltpu.VMEM)),
        scratch_shapes=[
            vm(512, 2048), pltpu.VMEM((512, 2048), BF16), vm(2048, 128),
            pltpu.VMEM((512, 2048), BF16), pltpu.VMEM((512, 2048), BF16), pltpu.VMEM((2048, 256), BF16),
            vm(G, 16, 128), vm(G, 16, 128), vm(G, 16, 128),
            vm(Z, 16, 128), vm(Z, 16, 128), vm(Z, 16, 128),
            vm(Z, 128, 128), vm(Y, 256, 128), vm(Z, 128, 128), vm(Y, 256, 128),
            vm(Y, 32, 128), vm(Z, 32, 128), vm(Y, 32, 128), vm(Z, 32, 128),
            vm(Z, Y, 32, 128), vm(Y, Z, 32, 128),
            vm(128, 256), vm(512, 128), vm(T, 8, 128), vm(Y, 8, 128), vm(Z, 8, 128),
            dma(9), dma(3), dma(2, G), dma(2, G), dma(8, Z), dma(8, Z), dma(5, Y), dma(5, Y),
        ],
        compiler_params=pltpu.CompilerParams(collective_id=0, has_side_effects=True, vmem_limit_bytes=28 << 20),
        cost_estimate=pl.CostEstimate(flops=1 << 31, bytes_accessed=8 << 20, transcendentals=0),
    )(mom, grad, q_in)
    right = right.reshape(2048, 128)
    n = 512
    wide = pl.BlockSpec((512, n), lambda i: (0, i))
    tall = pl.BlockSpec((n, 128), lambda i: (i, 0))
    whole = lambda rows: pl.BlockSpec((rows, 128), lambda i: (0, 0))
    weight_new, momentum_new, q_new = pl.pallas_call(
        finish,
        grid=(2048 // n,),
        out_shape=(
            jax.ShapeDtypeStruct((512, 2048), F32),
            jax.ShapeDtypeStruct((512, 2048), F32),
            jax.ShapeDtypeStruct((2048, 128), F32),
        ),
        in_specs=[wide, wide, wide, tall, whole(512), whole(8)],
        out_specs=(wide, wide, tall),
        compiler_params=pltpu.CompilerParams(vmem_limit_bytes=24 << 20),
        cost_estimate=pl.CostEstimate(flops=1 << 31, bytes_accessed=21 << 20, transcendentals=0),
    )(mom, grad, weight, right, basis, sq)
    return (weight_new, momentum_new[None], q_new)


def solution(mesh):
    placed = (P("fsdp", "tp"), P("rep", "fsdp", "tp"), P("rep", "fsdp", "tp"), P("tp", None))
    return jax.shard_map(
        shards,
        mesh=mesh,
        in_specs=placed,
        out_specs=(P("fsdp", "tp"), P("rep", "fsdp", "tp"), P("tp", None)),
        check_vma=False,
    )
```

```python
import jax
import jax.numpy as jnp
from jax import lax
from jax.experimental import pallas as pl
from jax.experimental.pallas import tpu as pltpu
from jax.sharding import PartitionSpec as P

MESH = pl.DeviceIdType.MESH
F32 = jnp.float32
BF16 = jnp.bfloat16
Z, T, Y = 8, 8, 4
G = T * Y


def split(x):
    hi = x.astype(BF16)
    return hi, (x - hi.astype(F32)).astype(BF16)


def mm(a, b, dims=((1,), (0,))):
    return lax.dot_general(a, b, (dims, ((), ())), preferred_element_type=F32)


def mmf(a, b, dims=((1,), (0,))):
    return lax.dot_general(a, b, (dims, ((), ())), precision=lax.Precision.HIGHEST, preferred_element_type=F32)


class Exchange:
    def __init__(self, n, me, device, src, dst, send, recv):
        self.n, self.me, self.device, self.src, self.dst = n, me, device, src, dst
        self.send, self.recv = send, recv

    def each(self, body):
        def step(o, carry):
            body(lax.rem(self.me + o, self.n))
            return carry

        lax.fori_loop(1, self.n, step, 0)

    def copy(self, j, slot):
        return pltpu.make_async_remote_copy(
            src_ref=self.src(j),
            dst_ref=self.dst(slot),
            send_sem=self.send.at[j],
            recv_sem=self.recv.at[slot],
            device_id=self.device(j),
            device_id_type=MESH,
        )

    def start(self):
        self.each(lambda j: self.copy(j, self.me).start())

    def wait_recv(self):
        self.each(lambda j: self.copy(j, j).wait_recv())

    def wait_send(self):
        self.each(lambda j: self.copy(j, self.me).wait_send())


def total(ref, n):
    acc = ref[0]
    for k in range(1, n):
        acc = acc + ref[k]
    return acc


def factor(work, gram):
    rows = lax.broadcasted_iota(jnp.int32, (128, 128), 0)
    lanes = lax.broadcasted_iota(jnp.int32, (128, 128), 1)
    lane = lanes[0:1]
    work[:, 0:128] = gram
    work[:, 128:256] = jnp.where(rows == lanes, 1.0, 0.0).astype(F32)
    for low in range(0, 128, 32):
        below = lax.broadcasted_iota(jnp.int32, (128 - low, 1), 0) + low
        wide = lanes[low:128]

        def step(k, carry):
            j = 4 * k
            row = [work[pl.ds(j + s, 1), :] for s in range(4)]
            left = work[low:128, 0:128]
            col = [jnp.sum(jnp.where(wide == j + s, left, 0.0), axis=1, keepdims=True) for s in range(4)]
            e = {}
            for a in range(4):
                for b in range(a, 4):
                    e[a, b] = jnp.sum(jnp.where(lane == j + b, row[a][:, 0:128], 0.0), axis=1, keepdims=True)
            update = None
            for a in range(4):
                inv = 1.0 / e[a, a]
                for b in range(a + 1, 4):
                    q = e[a, b] * inv
                    row[b] = row[b] - q * row[a]
                    for c in range(b, 4):
                        e[b, c] = e[b, c] - q * e[a, c]
                    col[b] = col[b] - q * col[a]
                term = jnp.where(below > j + 3, col[a] * inv, 0.0) * row[a]
                update = term if update is None else update + term
            work[low:128, :] = work[low:128, :] - update
            for a in range(1, 4):
                work[pl.ds(j + a, 1), :] = row[a]
            return carry

        lax.fori_loop(low // 4, low // 4 + 8, step, 0)
    d = jnp.sum(jnp.where(rows == lanes, work[:, 0:128], 0.0), axis=1, keepdims=True)
    return work[:, 128:256] * lax.rsqrt(d)


def talk(
    mom, grad, q_in, weight, right_out, basis_out, sq_out, buffer_out, weight_out,
    mom_v, grad_v, q_v, hi_v, lo_v, q_hl,
    part, part_r, proj, gram_p, gram_r, gram,
    wa, wb, ra1, rb1, sa1, sb1, ra2, rb2, rta, rtb,
    work, basis_v, sq_t, sq_y, sq_z,
    load, store, s_tp, r_tp, s_z, r_z, s_y, r_y,
):
    f, t, r = lax.axis_index("fsdp"), lax.axis_index("tp"), lax.axis_index("rep")
    g = t * Y + r

    loads = [pltpu.make_async_copy(q_in, q_v, load.at[8])]
    for c in range(4):
        cols = pl.ds(512 * c, 512)
        loads.append(pltpu.make_async_copy(mom.at[:, cols], mom_v.at[:, cols], load.at[2 * c]))
        loads.append(pltpu.make_async_copy(grad.at[:, cols], grad_v.at[:, cols], load.at[2 * c + 1]))
    for cp in loads:
        cp.start()
    keep_weight = pltpu.make_async_copy(weight, weight_out, load.at[9])

    plane = lambda j: {"tp": lax.div(j, Y), "rep": lax.rem(j, Y)}
    along_z = lambda j: {"fsdp": j}
    along_y = lambda j: {"rep": j}
    along_t = lambda j: {"tp": j}

    barrier = pltpu.get_barrier_semaphore()

    def greet(n, me, device):
        def step(o, carry):
            pl.semaphore_signal(barrier, inc=1, device_id=device(lax.rem(me + o, n)), device_id_type=MESH)
            return carry

        lax.fori_loop(1, n, step, 0)

    greet(G, g, plane)
    greet(Z, f, along_z)

    ex_part = Exchange(G, g, plane, lambda j: part.at[j], lambda i: part_r.at[i], s_tp.at[0], r_tp.at[0])
    ex_proj = Exchange(G, g, plane, lambda j: proj.at[g], lambda i: proj.at[i], s_tp.at[1], r_tp.at[1])
    ex_gram = Exchange(Z, f, along_z, lambda j: gram_p.at[j], lambda i: gram_r.at[i], s_z.at[0], r_z.at[0])
    ex_gall = Exchange(Z, f, along_z, lambda j: gram.at[f], lambda i: gram.at[i], s_z.at[1], r_z.at[1])
    ex_a1 = Exchange(Z, f, along_z, lambda j: wa.at[j], lambda i: ra1.at[i], s_z.at[2], r_z.at[2])
    ex_b1 = Exchange(Y, r, along_y, lambda j: wb.at[j], lambda i: rb1.at[i], s_y.at[0], r_y.at[0])
    ex_a2 = Exchange(Y, r, along_y, lambda j: sa1.at[j], lambda i: ra2.at[i], s_y.at[1], r_y.at[1])
    ex_b2 = Exchange(Z, f, along_z, lambda j: sb1.at[j], lambda i: rb2.at[i], s_z.at[3], r_z.at[3])
    ga1 = Exchange(Y, r, along_y, lambda j: rta.at[f, r], lambda i: rta.at[f, i], s_y.at[2], r_y.at[2])
    gb1 = Exchange(Z, f, along_z, lambda j: rtb.at[r, f], lambda i: rtb.at[r, i], s_z.at[4], r_z.at[4])
    ga2 = Exchange(Z, f, along_z, lambda j: rta.at[f], lambda i: rta.at[i], s_z.at[5], r_z.at[5])
    gb2 = Exchange(Y, r, along_y, lambda j: rtb.at[r], lambda i: rtb.at[i], s_y.at[3], r_y.at[3])
    ex_qt = Exchange(T, t, along_t, lambda j: sq_t.at[t], lambda i: sq_t.at[i], s_z.at[6], r_z.at[6])
    ex_qy = Exchange(Y, r, along_y, lambda j: sq_y.at[r], lambda i: sq_y.at[i], s_y.at[4], r_y.at[4])
    ex_qz = Exchange(Z, f, along_z, lambda j: sq_z.at[f], lambda i: sq_z.at[i], s_z.at[7], r_z.at[7])

    loads[0].wait()
    q_h, q_l = split(q_v[...])
    q_hl[:, 0:128] = q_h
    q_hl[:, 128:256] = q_l
    acc = None
    for c in range(4):
        cols = pl.ds(512 * c, 512)
        loads[2 * c + 1].wait()
        loads[2 * c + 2].wait()
        b = mom_v[:, cols] + grad_v[:, cols].astype(F32)
        mom_v[:, cols] = b
        b_h, b_l = split(b)
        hi_v[:, cols] = b_h
        lo_v[:, cols] = b_l
        both = mm(b_h, q_hl[cols, :])
        term = both[:, 0:128] + (both[:, 128:256] + mm(b_l, q_hl[cols, 0:128]))
        acc = term if acc is None else acc + term
    part[...] = acc.reshape(G, 16, 128)
    part_r[pl.ds(g, 1)] = part[pl.ds(g, 1)]

    pl.semaphore_wait(barrier, G + Z - 2)
    keep_weight.start()
    keep_buffer = pltpu.make_async_copy(mom_v, buffer_out, load.at[10])
    keep_buffer.start()
    ex_part.start()
    ex_part.wait_recv()
    proj[pl.ds(g, 1)] = total(part_r, G)[None]
    ex_proj.start()
    ex_proj.wait_recv()

    p = proj[...].reshape(512, 128)
    pt = p.T
    pt_h, pt_l = split(pt)
    gram_p[...] = mmf(pt, p).reshape(Z, 16, 128)
    gram_r[pl.ds(f, 1)] = gram_p[pl.ds(f, 1)]
    ex_gram.start()

    def columns(lo, n):
        b_h = hi_v[:, lo : lo + n]
        w = mm(pt_h, b_h) + (mm(pt_l, b_h) + mm(pt_h, lo_v[:, lo : lo + n]))
        return w.T

    for c in range(2):
        wa[4 * c : 4 * c + 4] = columns(384 * c, 384).reshape(4, 96, 128)
    ra1[pl.ds(f, 1)] = wa[pl.ds(f, 1)]
    ex_a1.start()
    for c in range(2):
        wb[2 * c : 2 * c + 2] = columns(768 + 640 * c, 640).reshape(2, 320, 128)
    rb1[pl.ds(r, 1)] = wb[pl.ds(r, 1)]
    ex_b1.start()

    ex_gram.wait_recv()
    gram[pl.ds(f, 1)] = total(gram_r, Z)[None]
    ex_gall.start()
    ex_b1.wait_recv()
    sb1[...] = total(rb1, Y).reshape(Z, 40, 128)
    rb2[pl.ds(f, 1)] = sb1[pl.ds(f, 1)]
    ex_b2.start()
    ex_gall.wait_recv()
    inverse = factor(work, gram[...].reshape(128, 128))
    ex_a1.wait_recv()
    sa1[...] = total(ra1, Z).reshape(Y, 24, 128)
    ra2[pl.ds(r, 1)] = sa1[pl.ds(r, 1)]
    ex_a2.start()
    basis_v[...] = mmf(p, inverse, ((1,), (1,)))
    keep_basis = pltpu.make_async_copy(basis_v, basis_out, store.at[0])
    keep_basis.start()
    ex_a2.wait_recv()
    ex_b2.wait_recv()
    w = jnp.concatenate([total(ra2, Y), total(rb2, Z)], axis=0)
    right = 0.25 * mmf(w, inverse, ((1,), (1,)))
    rta[pl.ds(f, 1), pl.ds(r, 1)] = right[0:24][None, None]
    rtb[pl.ds(r, 1), pl.ds(f, 1)] = right[24:64][None, None]
    ga1.start()
    gb1.start()
    squares = jnp.sum(right * right, axis=0, keepdims=True)
    sq_t[pl.ds(t, 1)] = jnp.broadcast_to(squares, (8, 128))[None]
    ex_qt.start()

    ex_qt.wait_recv()
    sq_y[pl.ds(r, 1)] = total(sq_t, T)[None]
    ex_qy.start()
    ga1.wait_recv()
    ga2.start()
    ex_qy.wait_recv()
    sq_z[pl.ds(f, 1)] = total(sq_y, Y)[None]
    ex_qz.start()
    gb1.wait_recv()
    gb2.start()
    ex_qz.wait_recv()
    sq_out[...] = total(sq_z, Z)
    gb2.wait_recv()
    keep_b = pltpu.make_async_copy(rtb.reshape(1280, 128), right_out.at[768:2048], store.at[1])
    keep_a = pltpu.make_async_copy(rta.reshape(768, 128), right_out.at[0:768], store.at[2])
    keep_b.start()
    ga2.wait_recv()
    keep_a.start()
    for ex in (ex_part, ex_proj, ex_gram, ex_gall, ex_a1, ex_b1, ex_a2, ex_b2, ga1, gb1, ga2, gb2, ex_qt, ex_qy, ex_qz):
        ex.wait_send()
    keep_weight.wait()
    keep_buffer.wait()
    keep_basis.wait()
    keep_b.wait()
    keep_a.wait()


def finish(buffer, weight, right, basis, sq, weight_out, mom_out, q_out):
    r = right[...]
    scale = lax.rsqrt(sq[0:1] * (1.0 / 16384.0) + 1e-06)
    q_out[...] = r * scale
    r_h, r_l = split(r)
    nt = ((1,), (1,))
    b = basis[...]
    b_h, b_l = split(b)
    feedback = mm(b_h, r_h, nt) + (mm(b_h, r_l, nt) + mm(b_l, r_h, nt))
    mom_out[...] = buffer[...] - 0.05 * feedback
    s_h, s_l = split(b * scale)
    update = mm(s_h, r_h, nt) + (mm(s_h, r_l, nt) + mm(s_l, r_h, nt))
    weight_out[...] = 0.999 * weight[...] - 0.2 * update


def shards(weight, momentum, gradient, q_in):
    mom, grad = momentum[0], gradient[0]
    vm = lambda *shape: pltpu.VMEM(shape, F32)
    dma = lambda *shape: pltpu.SemaphoreType.DMA(shape)
    any_ = pl.BlockSpec(memory_space=pl.ANY)
    hbm = pl.BlockSpec(memory_space=pltpu.HBM)
    right, basis, sq, buffer, weight = pl.pallas_call(
        talk,
        out_shape=(
            jax.ShapeDtypeStruct((2048, 128), F32),
            jax.ShapeDtypeStruct((512, 128), F32),
            jax.ShapeDtypeStruct((8, 128), F32),
            pltpu.VMEM((512, 2048), F32),
            pltpu.VMEM((512, 2048), F32),
        ),
        in_specs=[hbm] * 4,
        out_specs=(any_, any_, pl.BlockSpec(memory_space=pltpu.VMEM), any_, any_),
        scratch_shapes=[
            vm(512, 2048), pltpu.VMEM((512, 2048), BF16), vm(2048, 128),
            pltpu.VMEM((512, 2048), BF16), pltpu.VMEM((512, 2048), BF16), pltpu.VMEM((2048, 256), BF16),
            vm(G, 16, 128), vm(G, 16, 128), vm(G, 16, 128),
            vm(Z, 16, 128), vm(Z, 16, 128), vm(Z, 16, 128),
            vm(Z, 96, 128), vm(Y, 320, 128), vm(Z, 96, 128), vm(Y, 320, 128),
            vm(Y, 24, 128), vm(Z, 40, 128), vm(Y, 24, 128), vm(Z, 40, 128),
            vm(Z, Y, 24, 128), vm(Y, Z, 40, 128),
            vm(128, 256), vm(512, 128), vm(T, 8, 128), vm(Y, 8, 128), vm(Z, 8, 128),
            dma(11), dma(3), dma(2, G), dma(2, G), dma(8, Z), dma(8, Z), dma(5, Y), dma(5, Y),
        ],
        compiler_params=pltpu.CompilerParams(collective_id=0, has_side_effects=True, vmem_limit_bytes=28 << 20),
        cost_estimate=pl.CostEstimate(flops=1 << 31, bytes_accessed=8 << 20, transcendentals=0),
    )(*(pltpu.with_memory_space_constraint(x, pltpu.HBM) for x in (mom, grad, q_in, weight)))
    n = 512
    wide = pl.BlockSpec((512, n), lambda i: (0, i))
    tall = pl.BlockSpec((n, 128), lambda i: (i, 0))
    whole = lambda rows: pl.BlockSpec((rows, 128), lambda i: (0, 0))
    weight_new, momentum_new, q_new = pl.pallas_call(
        finish,
        grid=(2048 // n,),
        out_shape=(
            jax.ShapeDtypeStruct((512, 2048), F32),
            jax.ShapeDtypeStruct((512, 2048), F32),
            jax.ShapeDtypeStruct((2048, 128), F32),
        ),
        in_specs=[wide, wide, tall, whole(512), whole(8)],
        out_specs=(wide, wide, tall),
        compiler_params=pltpu.CompilerParams(vmem_limit_bytes=24 << 20),
        cost_estimate=pl.CostEstimate(flops=1 << 31, bytes_accessed=21 << 20, transcendentals=0),
    )(buffer, weight, right, basis, sq)
    return (weight_new, momentum_new[None], q_new)


def solution(mesh):
    placed = (P("fsdp", "tp"), P("rep", "fsdp", "tp"), P("rep", "fsdp", "tp"), P("tp", None))
    return jax.shard_map(
        shards,
        mesh=mesh,
        in_specs=placed,
        out_specs=(P("fsdp", "tp"), P("rep", "fsdp", "tp"), P("tp", None)),
        check_vma=False,
    )
```

```python
import jax
import jax.numpy as jnp
from jax import lax
from jax.experimental import pallas as pl
from jax.experimental.pallas import tpu as pltpu
from jax.sharding import PartitionSpec as P

MESH = pl.DeviceIdType.MESH
F32 = jnp.float32
BF16 = jnp.bfloat16
Z, T, Y = 8, 8, 4
G = T * Y


def split(x):
    hi = x.astype(BF16)
    return hi, (x - hi.astype(F32)).astype(BF16)


def mm(a, b, dims=((1,), (0,))):
    return lax.dot_general(a, b, (dims, ((), ())), preferred_element_type=F32)


def mmf(a, b, dims=((1,), (0,))):
    return lax.dot_general(a, b, (dims, ((), ())), precision=lax.Precision.HIGHEST, preferred_element_type=F32)


class Exchange:
    def __init__(self, n, me, device, src, dst, send, recv):
        self.n, self.me, self.device, self.src, self.dst = n, me, device, src, dst
        self.send, self.recv = send, recv

    def each(self, body):
        def step(o, carry):
            body(lax.rem(self.me + o, self.n))
            return carry

        lax.fori_loop(1, self.n, step, 0)

    def copy(self, j, slot):
        return pltpu.make_async_remote_copy(
            src_ref=self.src(j),
            dst_ref=self.dst(slot),
            send_sem=self.send.at[j],
            recv_sem=self.recv.at[slot],
            device_id=self.device(j),
            device_id_type=MESH,
        )

    def start_one(self, j):
        self.copy(j, self.me).start()

    def recv_one(self, j):
        self.copy(j, j).wait_recv()

    def start(self):
        self.each(lambda j: self.copy(j, self.me).start())

    def wait_recv(self):
        self.each(lambda j: self.copy(j, j).wait_recv())

    def wait_send(self):
        self.each(lambda j: self.copy(j, self.me).wait_send())


def total(ref, n):
    acc = ref[0]
    for k in range(1, n):
        acc = acc + ref[k]
    return acc


def factor(work, gram):
    rows = lax.broadcasted_iota(jnp.int32, (128, 128), 0)
    lanes = lax.broadcasted_iota(jnp.int32, (128, 128), 1)
    lane = lanes[0:1]
    work[:, 0:128] = gram
    work[:, 128:256] = jnp.where(rows == lanes, 1.0, 0.0).astype(F32)
    for low in range(0, 128, 32):
        below = lax.broadcasted_iota(jnp.int32, (128 - low, 1), 0) + low
        wide = lanes[low:128]

        def step(k, carry):
            j = 4 * k
            row = [work[pl.ds(j + s, 1), :] for s in range(4)]
            left = work[low:128, 0:128]
            col = [jnp.sum(jnp.where(wide == j + s, left, 0.0), axis=1, keepdims=True) for s in range(4)]
            e = {}
            for a in range(4):
                for b in range(a, 4):
                    e[a, b] = jnp.sum(jnp.where(lane == j + b, row[a][:, 0:128], 0.0), axis=1, keepdims=True)
            update = None
            for a in range(4):
                inv = 1.0 / e[a, a]
                for b in range(a + 1, 4):
                    q = e[a, b] * inv
                    row[b] = row[b] - q * row[a]
                    for c in range(b, 4):
                        e[b, c] = e[b, c] - q * e[a, c]
                    col[b] = col[b] - q * col[a]
                term = jnp.where(below > j + 3, col[a] * inv, 0.0) * row[a]
                update = term if update is None else update + term
            work[low:128, :] = work[low:128, :] - update
            for a in range(1, 4):
                work[pl.ds(j + a, 1), :] = row[a]
            return carry

        lax.fori_loop(low // 4, low // 4 + 8, step, 0)
        yield


def inverse_factor(work):
    rows = lax.broadcasted_iota(jnp.int32, (128, 128), 0)
    lanes = lax.broadcasted_iota(jnp.int32, (128, 128), 1)
    d = jnp.sum(jnp.where(rows == lanes, work[:, 0:128], 0.0), axis=1, keepdims=True)
    return work[:, 128:256] * lax.rsqrt(d)


def talk(
    mom, grad, q_in, weight, right_out, basis_out, sq_out, buffer_out, weight_out,
    mom_v, grad_v, q_v, hi_v, lo_v, q_hl,
    part, part_r, proj, gram_p, gram_r, gram,
    wa, wb, ra1, rb1, sa1, sb1, ra2, rb2, rta, rtb,
    work, basis_v, sq_t, sq_y, sq_z,
    load, store, s_tp, r_tp, s_z, r_z, s_y, r_y, s_pa, r_pa, s_pb, r_pb,
):
    f, t, r = lax.axis_index("fsdp"), lax.axis_index("tp"), lax.axis_index("rep")
    g = t * Y + r

    loads = [pltpu.make_async_copy(q_in, q_v, load.at[8])]
    for c in range(4):
        cols = pl.ds(512 * c, 512)
        loads.append(pltpu.make_async_copy(mom.at[:, cols], mom_v.at[:, cols], load.at[2 * c]))
        loads.append(pltpu.make_async_copy(grad.at[:, cols], grad_v.at[:, cols], load.at[2 * c + 1]))
    for cp in loads:
        cp.start()
    keep_weight = pltpu.make_async_copy(weight, weight_out, load.at[9])

    plane = lambda j: {"tp": lax.div(j, Y), "rep": lax.rem(j, Y)}
    along_z = lambda j: {"fsdp": j}
    along_y = lambda j: {"rep": j}
    along_t = lambda j: {"tp": j}

    barrier = pltpu.get_barrier_semaphore()

    def greet(n, me, device):
        def step(o, carry):
            pl.semaphore_signal(barrier, inc=1, device_id=device(lax.rem(me + o, n)), device_id_type=MESH)
            return carry

        lax.fori_loop(1, n, step, 0)

    greet(G, g, plane)
    greet(Z, f, along_z)

    ex_part = Exchange(G, g, plane, lambda j: part.at[j], lambda i: part_r.at[i], s_tp.at[0], r_tp.at[0])
    ex_proj = Exchange(G, g, plane, lambda j: proj.at[g], lambda i: proj.at[i], s_tp.at[1], r_tp.at[1])
    ex_gram = Exchange(Z, f, along_z, lambda j: gram_p.at[j], lambda i: gram_r.at[i], s_z.at[0], r_z.at[0])
    ex_gall = Exchange(Z, f, along_z, lambda j: gram.at[f], lambda i: gram.at[i], s_z.at[1], r_z.at[1])
    ex_a2 = Exchange(Y, r, along_y, lambda j: sa1.at[j], lambda i: ra2.at[i], s_y.at[0], r_y.at[0])
    ex_b2 = Exchange(Z, f, along_z, lambda j: sb1.at[j], lambda i: rb2.at[i], s_z.at[2], r_z.at[2])

    def ex_a1(p):
        return Exchange(Z, f, along_z, lambda j: wa.at[j, p], lambda i: ra1.at[i, p], s_pa.at[0, p], r_pa.at[0, p])

    def ex_b1(p):
        return Exchange(Y, r, along_y, lambda j: wb.at[j, p], lambda i: rb1.at[i, p], s_pb.at[0, p], r_pb.at[0, p])

    ga1 = Exchange(Y, r, along_y, lambda j: rta.at[f, r], lambda i: rta.at[f, i], s_y.at[1], r_y.at[1])
    gb1 = Exchange(Z, f, along_z, lambda j: rtb.at[r, f], lambda i: rtb.at[r, i], s_z.at[3], r_z.at[3])

    def ga2(p):
        return Exchange(Z, f, along_z, lambda j: rta.at[f, p], lambda i: rta.at[i, p], s_pa.at[1, p], r_pa.at[1, p])

    def gb2(p):
        return Exchange(Y, r, along_y, lambda j: rtb.at[r, p], lambda i: rtb.at[i, p], s_pb.at[1, p], r_pb.at[1, p])

    ex_qt = Exchange(T, t, along_t, lambda j: sq_t.at[t], lambda i: sq_t.at[i], s_z.at[4], r_z.at[4])
    ex_qy = Exchange(Y, r, along_y, lambda j: sq_y.at[r], lambda i: sq_y.at[i], s_y.at[2], r_y.at[2])
    ex_qz = Exchange(Z, f, along_z, lambda j: sq_z.at[f], lambda i: sq_z.at[i], s_z.at[5], r_z.at[5])

    loads[0].wait()
    q_h, q_l = split(q_v[...])
    q_hl[:, 0:128] = q_h
    q_hl[:, 128:256] = q_l
    acc = None
    for c in range(4):
        cols = pl.ds(512 * c, 512)
        loads[2 * c + 1].wait()
        loads[2 * c + 2].wait()
        b = mom_v[:, cols] + grad_v[:, cols].astype(F32)
        mom_v[:, cols] = b
        b_h, b_l = split(b)
        hi_v[:, cols] = b_h
        lo_v[:, cols] = b_l
        both = mm(b_h, q_hl[cols, :])
        term = both[:, 0:128] + (both[:, 128:256] + mm(b_l, q_hl[cols, 0:128]))
        acc = term if acc is None else acc + term
    part[...] = acc.reshape(G, 16, 128)
    part_r[pl.ds(g, 1)] = part[pl.ds(g, 1)]

    pl.semaphore_wait(barrier, G + Z - 2)
    keep_weight.start()
    keep_buffer = pltpu.make_async_copy(mom_v, buffer_out, load.at[10])
    keep_buffer.start()
    ex_part.start()
    ex_part.wait_recv()
    proj[pl.ds(g, 1)] = total(part_r, G)[None]
    ex_proj.start()
    ex_proj.wait_recv()

    p_all = proj[...].reshape(512, 128)
    pt = p_all.T
    pt_h, pt_l = split(pt)
    gram_p[...] = mmf(pt, p_all).reshape(Z, 16, 128)
    gram_r[pl.ds(f, 1)] = gram_p[pl.ds(f, 1)]
    ex_gram.start()

    def columns(lo, n):
        b_h = hi_v[:, lo : lo + n]
        w = mm(pt_h, b_h) + (mm(pt_l, b_h) + mm(pt_h, lo_v[:, lo : lo + n]))
        return w.T

    order_a = [lax.rem(r + o, Y) for o in (2, 1, 3, 0)]
    order_b = [lax.rem(f + o, Z) for o in (4, 3, 5, 2, 6, 1, 7, 0)]

    def take_a(p, last=False):
        ex_a1(p).wait_recv()
        acc = wa[f, p]
        for o in range(1, Z):
            acc = acc + ra1[lax.rem(f + o, Z), p]
        if last:
            return acc
        sa1[p] = acc
        ex_a2.start_one(p)

    def take_b(p, last=False):
        ex_b1(p).wait_recv()
        acc = wb[r, p]
        for o in range(1, Y):
            acc = acc + rb1[lax.rem(r + o, Y), p]
        if last:
            return acc
        sb1[p] = acc
        ex_b2.start_one(p)

    wa[...] = columns(0, 512).reshape(Z, Y, 16, 128)
    for p in order_a[0:2]:
        ex_a1(p).start()
    for c in range(2):
        wb[2 * c : 2 * c + 2] = columns(512 + 768 * c, 768).reshape(2, Z, 48, 128)
    for p in order_b:
        ex_b1(p).start()
    ex_gram.wait_recv()
    gram[pl.ds(f, 1)] = total(gram_r, Z)[None]
    ex_gall.start()
    for p in order_a[2:4]:
        ex_a1(p).start()

    for p in order_b[0:2]:
        take_b(p)
    take_a(order_a[0])
    take_b(order_b[2])
    ex_gall.wait_recv()
    steps = factor(work, gram[...].reshape(128, 128))
    next(steps)
    take_b(order_b[3])
    take_b(order_b[4])
    take_a(order_a[1])
    next(steps)
    take_b(order_b[5])
    take_a(order_a[2])
    next(steps)
    take_b(order_b[6])
    own_a = take_a(order_a[3], last=True)
    next(steps)
    own_b = take_b(order_b[7], last=True)
    inverse = inverse_factor(work)

    ex_a2.wait_recv()
    for o in range(1, Y):
        own_a = own_a + ra2[lax.rem(r + o, Y)]
    ex_b2.wait_recv()
    for o in range(1, Z):
        own_b = own_b + rb2[lax.rem(f + o, Z)]
    w = jnp.concatenate([own_a, own_b], axis=0)
    right = 0.25 * mmf(w, inverse, ((1,), (1,)))
    rta[f, r] = right[0:16]
    rtb[r, f] = right[16:64]
    gb1.start()
    ga1.start()
    squares = jnp.sum(right * right, axis=0, keepdims=True)
    sq_t[t] = jnp.broadcast_to(squares, (8, 128))
    ex_qt.start()
    gb2(f).start()
    ga2(r).start()

    def forward_b(o):
        p = lax.rem(f + o, Z)
        gb1.recv_one(p)
        gb2(p).start()

    for o in (1, 7):
        forward_b(o)
    for o in range(1, Y):
        p = lax.rem(r + o, Y)
        ga1.recv_one(p)
        ga2(p).start()
    ex_qt.wait_recv()
    sq_y[r] = total(sq_t, T)
    ex_qy.start()
    for o in (2, 6, 3, 5, 4):
        forward_b(o)
    ex_qy.wait_recv()
    sq_z[f] = total(sq_y, Y)
    ex_qz.start()
    basis_v[...] = mmf(proj[...].reshape(512, 128), inverse, ((1,), (1,)))
    keep_basis = pltpu.make_async_copy(basis_v, basis_out, store.at[0])
    keep_basis.start()
    for o in range(Z):
        gb2(lax.rem(f + o, Z)).wait_recv()
    keep_b = pltpu.make_async_copy(rtb.reshape(1536, 128), right_out.at[512:2048], store.at[1])
    keep_b.start()
    for o in range(Y):
        ga2(lax.rem(r + o, Y)).wait_recv()
    keep_a = pltpu.make_async_copy(rta.reshape(512, 128), right_out.at[0:512], store.at[2])
    keep_a.start()
    ex_qz.wait_recv()
    sq_out[...] = total(sq_z, Z)
    for ex in (ex_part, ex_proj, ex_gram, ex_gall, ex_a2, ex_b2, ga1, gb1, ex_qt, ex_qy, ex_qz):
        ex.wait_send()

    def sent_a(p, carry):
        ex_a1(p).wait_send()
        ga2(p).wait_send()
        return carry

    def sent_b(p, carry):
        ex_b1(p).wait_send()
        gb2(p).wait_send()
        return carry

    lax.fori_loop(0, Y, sent_a, 0)
    lax.fori_loop(0, Z, sent_b, 0)
    keep_weight.wait()
    keep_buffer.wait()
    keep_basis.wait()
    keep_b.wait()
    keep_a.wait()


def finish(buffer, weight, right, basis, sq, weight_out, mom_out, q_out, w_v, m_v, q_v, sem_w, sem_m, sem_q):
    scale = lax.rsqrt(sq[0:1] * (1.0 / 16384.0) + 1e-06)
    nt = ((1,), (1,))
    b = basis[...]
    b_h, b_l = split(b)
    s_h, s_l = split(b * scale)
    copies = []
    for c in range(8):
        cols = pl.ds(256 * c, 256)
        r = right[cols, :]
        r_h, r_l = split(r)
        feedback = mm(b_h, r_h, nt) + (mm(b_h, r_l, nt) + mm(b_l, r_h, nt))
        m_v[:, cols] = buffer[:, cols] - 0.05 * feedback
        copies.append(pltpu.make_async_copy(m_v.at[:, cols], mom_out.at[:, cols], sem_m.at[c]))
        copies[-1].start()
        update = mm(s_h, r_h, nt) + (mm(s_h, r_l, nt) + mm(s_l, r_h, nt))
        w_v[:, cols] = 0.999 * weight[:, cols] - 0.2 * update
        copies.append(pltpu.make_async_copy(w_v.at[:, cols], weight_out.at[:, cols], sem_w.at[c]))
        copies[-1].start()
        q_v[cols, :] = r * scale
        copies.append(pltpu.make_async_copy(q_v.at[cols, :], q_out.at[cols, :], sem_q.at[c]))
        copies[-1].start()
    for cp in copies:
        cp.wait()


def shards(weight, momentum, gradient, q_in):
    mom, grad = momentum[0], gradient[0]
    vm = lambda *shape: pltpu.VMEM(shape, F32)
    dma = lambda *shape: pltpu.SemaphoreType.DMA(shape)
    any_ = pl.BlockSpec(memory_space=pl.ANY)
    hbm = pl.BlockSpec(memory_space=pltpu.HBM)
    right, basis, sq, buffer, weight = pl.pallas_call(
        talk,
        out_shape=(
            jax.ShapeDtypeStruct((2048, 128), F32),
            jax.ShapeDtypeStruct((512, 128), F32),
            jax.ShapeDtypeStruct((8, 128), F32),
            pltpu.VMEM((512, 2048), F32),
            pltpu.VMEM((512, 2048), F32),
        ),
        in_specs=[hbm] * 4,
        out_specs=(any_, any_, pl.BlockSpec(memory_space=pltpu.VMEM), any_, any_),
        scratch_shapes=[
            vm(512, 2048), pltpu.VMEM((512, 2048), BF16), vm(2048, 128),
            pltpu.VMEM((512, 2048), BF16), pltpu.VMEM((512, 2048), BF16), pltpu.VMEM((2048, 256), BF16),
            vm(G, 16, 128), vm(G, 16, 128), vm(G, 16, 128),
            vm(Z, 16, 128), vm(Z, 16, 128), vm(Z, 16, 128),
            vm(Z, Y, 16, 128), vm(Y, Z, 48, 128), vm(Z, Y, 16, 128), vm(Y, Z, 48, 128),
            vm(Y, 16, 128), vm(Z, 48, 128), vm(Y, 16, 128), vm(Z, 48, 128),
            vm(Z, Y, 16, 128), vm(Y, Z, 48, 128),
            vm(128, 256), vm(512, 128), vm(T, 8, 128), vm(Y, 8, 128), vm(Z, 8, 128),
            dma(11), dma(3), dma(2, G), dma(2, G), dma(6, Z), dma(6, Z), dma(3, Y), dma(3, Y),
            dma(2, Y, Z), dma(2, Y, Z), dma(2, Z, Y), dma(2, Z, Y),
        ],
        compiler_params=pltpu.CompilerParams(collective_id=0, has_side_effects=True, vmem_limit_bytes=28 << 20),
        cost_estimate=pl.CostEstimate(flops=1 << 31, bytes_accessed=8 << 20, transcendentals=0),
    )(*(pltpu.with_memory_space_constraint(x, pltpu.HBM) for x in (mom, grad, q_in, weight)))
    weight_new, momentum_new, q_new = pl.pallas_call(
        finish,
        out_shape=(
            jax.ShapeDtypeStruct((512, 2048), F32),
            jax.ShapeDtypeStruct((512, 2048), F32),
            jax.ShapeDtypeStruct((2048, 128), F32),
        ),
        in_specs=[pl.BlockSpec(memory_space=pltpu.VMEM)] * 5,
        out_specs=(any_, any_, any_),
        scratch_shapes=[vm(512, 2048), vm(512, 2048), vm(2048, 128), dma(8), dma(8), dma(8)],
        compiler_params=pltpu.CompilerParams(vmem_limit_bytes=24 << 20),
        cost_estimate=pl.CostEstimate(flops=1 << 31, bytes_accessed=21 << 20, transcendentals=0),
    )(buffer, weight, right, basis, sq)
    return (weight_new, momentum_new[None], q_new)


def solution(mesh):
    placed = (P("fsdp", "tp"), P("rep", "fsdp", "tp"), P("rep", "fsdp", "tp"), P("tp", None))
    return jax.shard_map(
        shards,
        mesh=mesh,
        in_specs=placed,
        out_specs=(P("fsdp", "tp"), P("rep", "fsdp", "tp"), P("tp", None)),
        check_vma=False,
    )
```

```python
import jax
import jax.numpy as jnp
from jax import lax
from jax.experimental import pallas as pl
from jax.experimental.pallas import tpu as pltpu
from jax.sharding import PartitionSpec as P

MESH = pl.DeviceIdType.MESH
F32 = jnp.float32
BF16 = jnp.bfloat16
Z, T, Y = 8, 8, 4
G = T * Y


def split(x):
    hi = x.astype(BF16)
    return hi, (x - hi.astype(F32)).astype(BF16)


def mm(a, b, dims=((1,), (0,))):
    return lax.dot_general(a, b, (dims, ((), ())), preferred_element_type=F32)


def mmf(a, b, dims=((1,), (0,))):
    return lax.dot_general(a, b, (dims, ((), ())), precision=lax.Precision.HIGHEST, preferred_element_type=F32)


class Exchange:
    def __init__(self, n, me, device, src, dst, send, recv):
        self.n, self.me, self.device, self.src, self.dst = n, me, device, src, dst
        self.send, self.recv = send, recv

    def each(self, body):
        def step(o, carry):
            body(lax.rem(self.me + o, self.n))
            return carry

        lax.fori_loop(1, self.n, step, 0, unroll=True)

    def copy(self, j, slot):
        return pltpu.make_async_remote_copy(
            src_ref=self.src(j),
            dst_ref=self.dst(slot),
            send_sem=self.send.at[j],
            recv_sem=self.recv.at[slot],
            device_id=self.device(j),
            device_id_type=MESH,
        )

    def start_one(self, j):
        self.copy(j, self.me).start()

    def recv_one(self, j):
        self.copy(j, j).wait_recv()

    def start(self):
        self.each(lambda j: self.copy(j, self.me).start())

    def wait_recv(self):
        self.each(lambda j: self.copy(j, j).wait_recv())

    def wait_send(self):
        self.each(lambda j: self.copy(j, self.me).wait_send())


def total(ref, n):
    acc = ref[0]
    for k in range(1, n):
        acc = acc + ref[k]
    return acc


def factor(work, gram):
    rows = lax.broadcasted_iota(jnp.int32, (128, 128), 0)
    lanes = lax.broadcasted_iota(jnp.int32, (128, 128), 1)
    lane = lanes[0:1]
    work[:, 0:128] = gram
    work[:, 128:256] = jnp.where(rows == lanes, 1.0, 0.0).astype(F32)
    for low in range(0, 128, 32):
        below = lax.broadcasted_iota(jnp.int32, (128 - low, 1), 0) + low
        wide = lanes[low:128]

        def step(k, carry):
            j = 4 * k
            row = [work[pl.ds(j + s, 1), :] for s in range(4)]
            left = work[low:128, 0:128]
            col = [jnp.sum(jnp.where(wide == j + s, left, 0.0), axis=1, keepdims=True) for s in range(4)]
            e = {}
            for a in range(4):
                for b in range(a, 4):
                    e[a, b] = jnp.sum(jnp.where(lane == j + b, row[a][:, 0:128], 0.0), axis=1, keepdims=True)
            update = None
            for a in range(4):
                inv = 1.0 / e[a, a]
                for b in range(a + 1, 4):
                    q = e[a, b] * inv
                    row[b] = row[b] - q * row[a]
                    for c in range(b, 4):
                        e[b, c] = e[b, c] - q * e[a, c]
                    col[b] = col[b] - q * col[a]
                term = jnp.where(below > j + 3, col[a] * inv, 0.0) * row[a]
                update = term if update is None else update + term
            work[low:128, :] = work[low:128, :] - update
            for a in range(1, 4):
                work[pl.ds(j + a, 1), :] = row[a]
            return carry

        lax.fori_loop(low // 4, low // 4 + 8, step, 0)
        yield


def inverse_factor(work):
    rows = lax.broadcasted_iota(jnp.int32, (128, 128), 0)
    lanes = lax.broadcasted_iota(jnp.int32, (128, 128), 1)
    d = jnp.sum(jnp.where(rows == lanes, work[:, 0:128], 0.0), axis=1, keepdims=True)
    return work[:, 128:256] * lax.rsqrt(d)


def talk(
    mom, grad, q_in, weight, right_out, basis_out, sq_out, buffer_out, weight_out,
    mom_v, grad_v, q_v, hi_v, lo_v, q_hl,
    part, part_r, proj, gram_p, gram_r, gram,
    wa, wb, ra1, rb1, sa1, sb1, ra2, rb2, rta, rtb,
    work, basis_v, sq_p, sq_z,
    load, store, s_tp, r_tp, s_z, r_z, s_y, r_y, s_pa, r_pa, s_pb, r_pb,
):
    f, t, r = lax.axis_index("fsdp"), lax.axis_index("tp"), lax.axis_index("rep")
    g = t * Y + r

    loads = [pltpu.make_async_copy(q_in, q_v, load.at[8])]
    for c in range(4):
        cols = pl.ds(512 * c, 512)
        loads.append(pltpu.make_async_copy(mom.at[:, cols], mom_v.at[:, cols], load.at[2 * c]))
        loads.append(pltpu.make_async_copy(grad.at[:, cols], grad_v.at[:, cols], load.at[2 * c + 1]))
    for cp in loads:
        cp.start()
    keep_weight = pltpu.make_async_copy(weight, weight_out, load.at[9])

    plane = lambda j: {"tp": lax.div(j, Y), "rep": lax.rem(j, Y)}
    along_z = lambda j: {"fsdp": j}
    along_y = lambda j: {"rep": j}

    barrier = pltpu.get_barrier_semaphore()

    def greet(n, me, device):
        def step(o, carry):
            pl.semaphore_signal(barrier, inc=1, device_id=device(lax.rem(me + o, n)), device_id_type=MESH)
            return carry

        lax.fori_loop(1, n, step, 0)

    greet(G, g, plane)
    greet(Z, f, along_z)

    ex_part = Exchange(G, g, plane, lambda j: part.at[j], lambda i: part_r.at[i], s_tp.at[0], r_tp.at[0])
    ex_proj = Exchange(G, g, plane, lambda j: proj.at[g], lambda i: proj.at[i], s_tp.at[1], r_tp.at[1])
    ex_gram = Exchange(Z, f, along_z, lambda j: gram_p.at[j], lambda i: gram_r.at[i], s_z.at[0], r_z.at[0])
    ex_gall = Exchange(Z, f, along_z, lambda j: gram.at[f], lambda i: gram.at[i], s_z.at[1], r_z.at[1])
    ex_a2 = Exchange(Y, r, along_y, lambda j: sa1.at[j], lambda i: ra2.at[i], s_y.at[0], r_y.at[0])
    ex_b2 = Exchange(Z, f, along_z, lambda j: sb1.at[j], lambda i: rb2.at[i], s_z.at[2], r_z.at[2])

    def ex_a1(p):
        return Exchange(Z, f, along_z, lambda j: wa.at[j, p], lambda i: ra1.at[i, p], s_pa.at[0, p], r_pa.at[0, p])

    def ex_b1(p):
        return Exchange(Y, r, along_y, lambda j: wb.at[j, p], lambda i: rb1.at[i, p], s_pb.at[0, p], r_pb.at[0, p])

    ga1 = Exchange(Y, r, along_y, lambda j: rta.at[f, r], lambda i: rta.at[f, i], s_y.at[1], r_y.at[1])
    gb1 = Exchange(Z, f, along_z, lambda j: rtb.at[r, f], lambda i: rtb.at[r, i], s_z.at[3], r_z.at[3])

    def ga2(p):
        return Exchange(Z, f, along_z, lambda j: rta.at[f, p], lambda i: rta.at[i, p], s_pa.at[1, p], r_pa.at[1, p])

    def gb2(p):
        return Exchange(Y, r, along_y, lambda j: rtb.at[r, p], lambda i: rtb.at[i, p], s_pb.at[1, p], r_pb.at[1, p])

    ex_qp = Exchange(G, g, plane, lambda j: sq_p.at[g], lambda i: sq_p.at[i], s_tp.at[2], r_tp.at[2])
    ex_qz = Exchange(Z, f, along_z, lambda j: sq_z.at[f], lambda i: sq_z.at[i], s_z.at[4], r_z.at[4])

    loads[0].wait()
    q_h, q_l = split(q_v[...])
    q_hl[:, 0:128] = q_h
    q_hl[:, 128:256] = q_l
    acc = None
    for c in range(4):
        cols = pl.ds(512 * c, 512)
        loads[2 * c + 1].wait()
        loads[2 * c + 2].wait()
        b = mom_v[:, cols] + grad_v[:, cols].astype(F32)
        mom_v[:, cols] = b
        b_h, b_l = split(b)
        hi_v[:, cols] = b_h
        lo_v[:, cols] = b_l
        both = mm(b_h, q_hl[cols, :])
        term = both[:, 0:128] + (both[:, 128:256] + mm(b_l, q_hl[cols, 0:128]))
        acc = term if acc is None else acc + term
    part[...] = acc.reshape(G, 16, 128)
    part_r[pl.ds(g, 1)] = part[pl.ds(g, 1)]

    pl.semaphore_wait(barrier, G + Z - 2)
    keep_weight.start()
    keep_buffer = pltpu.make_async_copy(mom_v, buffer_out, load.at[10])
    keep_buffer.start()
    ex_part.start()
    ex_part.wait_recv()
    proj[pl.ds(g, 1)] = total(part_r, G)[None]
    ex_proj.start()
    ex_proj.wait_recv()

    p_all = proj[...].reshape(512, 128)
    pt = p_all.T
    pt_h, pt_l = split(pt)
    gram_p[...] = mmf(pt, p_all).reshape(Z, 16, 128)
    gram_r[pl.ds(f, 1)] = gram_p[pl.ds(f, 1)]
    ex_gram.start()

    def columns(lo, n):
        b_h = hi_v[:, lo : lo + n]
        w = mm(pt_h, b_h) + (mm(pt_l, b_h) + mm(pt_h, lo_v[:, lo : lo + n]))
        return w.T

    order_a = [lax.rem(r + o, Y) for o in (2, 1, 3, 0)]
    order_b = [lax.rem(f + o, Z) for o in (4, 3, 5, 2, 6, 1, 7, 0)]

    def take_a(p, last=False):
        ex_a1(p).wait_recv()
        acc = wa[f, p]
        for o in range(1, Z):
            acc = acc + ra1[lax.rem(f + o, Z), p]
        if last:
            return acc
        sa1[p] = acc
        ex_a2.start_one(p)

    def take_b(p, last=False):
        ex_b1(p).wait_recv()
        acc = wb[r, p]
        for o in range(1, Y):
            acc = acc + rb1[lax.rem(r + o, Y), p]
        if last:
            return acc
        sb1[p] = acc
        ex_b2.start_one(p)

    wa[...] = columns(0, 512).reshape(Z, Y, 16, 128)
    for p in order_a[0:2]:
        ex_a1(p).start()
    for c in range(2):
        wb[2 * c : 2 * c + 2] = columns(512 + 768 * c, 768).reshape(2, Z, 48, 128)
    for p in order_b:
        ex_b1(p).start()
    ex_gram.wait_recv()
    gram[pl.ds(f, 1)] = total(gram_r, Z)[None]
    ex_gall.start()
    for p in order_a[2:4]:
        ex_a1(p).start()

    for p in order_b[0:2]:
        take_b(p)
    take_a(order_a[0])
    take_b(order_b[2])
    ex_gall.wait_recv()
    steps = factor(work, gram[...].reshape(128, 128))
    next(steps)
    take_b(order_b[3])
    take_b(order_b[4])
    take_a(order_a[1])
    next(steps)
    take_b(order_b[5])
    take_a(order_a[2])
    next(steps)
    take_b(order_b[6])
    own_a = take_a(order_a[3], last=True)
    next(steps)
    own_b = take_b(order_b[7], last=True)
    inverse = inverse_factor(work)

    ex_a2.wait_recv()
    for o in range(1, Y):
        own_a = own_a + ra2[lax.rem(r + o, Y)]
    ex_b2.wait_recv()
    for o in range(1, Z):
        own_b = own_b + rb2[lax.rem(f + o, Z)]
    w = jnp.concatenate([own_a, own_b], axis=0)
    right = 0.25 * mmf(w, inverse, ((1,), (1,)))
    rta[f, r] = right[0:16]
    rtb[r, f] = right[16:64]
    gb1.start()
    ga1.start()
    squares = jnp.sum(right * right, axis=0, keepdims=True)
    sq_p[g] = jnp.broadcast_to(squares, (8, 128))
    ex_qp.start()
    gb2(f).start()
    ga2(r).start()

    def forward_b(o):
        p = lax.rem(f + o, Z)
        gb1.recv_one(p)
        gb2(p).start()

    def forward_a(o):
        p = lax.rem(r + o, Y)
        ga1.recv_one(p)
        ga2(p).start()

    for o in (1, 7):
        forward_b(o)
    forward_a(1)
    forward_a(3)
    forward_a(2)
    forward_b(2)
    forward_b(6)
    ex_qp.wait_recv()
    sq_z[f] = total(sq_p, G)
    ex_qz.start()
    for o in (3, 5, 4):
        forward_b(o)
    basis_v[...] = mmf(proj[...].reshape(512, 128), inverse, ((1,), (1,)))
    keep_basis = pltpu.make_async_copy(basis_v, basis_out, store.at[0])
    keep_basis.start()
    for o in range(Z):
        gb2(lax.rem(f + o, Z)).wait_recv()
    keep_b = pltpu.make_async_copy(rtb.reshape(1536, 128), right_out.at[512:2048], store.at[1])
    keep_b.start()
    for o in range(Y):
        ga2(lax.rem(r + o, Y)).wait_recv()
    keep_a = pltpu.make_async_copy(rta.reshape(512, 128), right_out.at[0:512], store.at[2])
    keep_a.start()
    ex_qz.wait_recv()
    sq_out[...] = total(sq_z, Z)
    for ex in (ex_part, ex_proj, ex_gram, ex_gall, ex_a2, ex_b2, ga1, gb1, ex_qp, ex_qz):
        ex.wait_send()

    def sent_a(p, carry):
        ex_a1(p).wait_send()
        ga2(p).wait_send()
        return carry

    def sent_b(p, carry):
        ex_b1(p).wait_send()
        gb2(p).wait_send()
        return carry

    lax.fori_loop(0, Y, sent_a, 0)
    lax.fori_loop(0, Z, sent_b, 0)
    keep_weight.wait()
    keep_buffer.wait()
    keep_basis.wait()
    keep_b.wait()
    keep_a.wait()


def finish(buffer, weight, right, basis, sq, weight_out, mom_out, q_out, w_v, m_v, q_v, sem_w, sem_m, sem_q):
    scale = lax.rsqrt(sq[0:1] * (1.0 / 16384.0) + 1e-06)
    nt = ((1,), (1,))
    b = basis[...]
    b_h, b_l = split(b)
    s_h, s_l = split(b * scale)
    copies = []
    for c in range(8):
        cols = pl.ds(256 * c, 256)
        r = right[cols, :]
        r_h, r_l = split(r)
        feedback = mm(b_h, r_h, nt) + (mm(b_h, r_l, nt) + mm(b_l, r_h, nt))
        m_v[:, cols] = buffer[:, cols] - 0.05 * feedback
        copies.append(pltpu.make_async_copy(m_v.at[:, cols], mom_out.at[:, cols], sem_m.at[c]))
        copies[-1].start()
        update = mm(s_h, r_h, nt) + (mm(s_h, r_l, nt) + mm(s_l, r_h, nt))
        w_v[:, cols] = 0.999 * weight[:, cols] - 0.2 * update
        copies.append(pltpu.make_async_copy(w_v.at[:, cols], weight_out.at[:, cols], sem_w.at[c]))
        copies[-1].start()
        q_v[cols, :] = r * scale
        copies.append(pltpu.make_async_copy(q_v.at[cols, :], q_out.at[cols, :], sem_q.at[c]))
        copies[-1].start()
    for cp in copies:
        cp.wait()


def shards(weight, momentum, gradient, q_in):
    mom, grad = momentum[0], gradient[0]
    vm = lambda *shape: pltpu.VMEM(shape, F32)
    dma = lambda *shape: pltpu.SemaphoreType.DMA(shape)
    any_ = pl.BlockSpec(memory_space=pl.ANY)
    hbm = pl.BlockSpec(memory_space=pltpu.HBM)
    right, basis, sq, buffer, weight = pl.pallas_call(
        talk,
        out_shape=(
            jax.ShapeDtypeStruct((2048, 128), F32),
            jax.ShapeDtypeStruct((512, 128), F32),
            jax.ShapeDtypeStruct((8, 128), F32),
            pltpu.VMEM((512, 2048), F32),
            pltpu.VMEM((512, 2048), F32),
        ),
        in_specs=[hbm] * 4,
        out_specs=(any_, any_, pl.BlockSpec(memory_space=pltpu.VMEM), any_, any_),
        scratch_shapes=[
            vm(512, 2048), pltpu.VMEM((512, 2048), BF16), vm(2048, 128),
            pltpu.VMEM((512, 2048), BF16), pltpu.VMEM((512, 2048), BF16), pltpu.VMEM((2048, 256), BF16),
            vm(G, 16, 128), vm(G, 16, 128), vm(G, 16, 128),
            vm(Z, 16, 128), vm(Z, 16, 128), vm(Z, 16, 128),
            vm(Z, Y, 16, 128), vm(Y, Z, 48, 128), vm(Z, Y, 16, 128), vm(Y, Z, 48, 128),
            vm(Y, 16, 128), vm(Z, 48, 128), vm(Y, 16, 128), vm(Z, 48, 128),
            vm(Z, Y, 16, 128), vm(Y, Z, 48, 128),
            vm(128, 256), vm(512, 128), vm(G, 8, 128), vm(Z, 8, 128),
            dma(11), dma(3), dma(3, G), dma(3, G), dma(5, Z), dma(5, Z), dma(2, Y), dma(2, Y),
            dma(2, Y, Z), dma(2, Y, Z), dma(2, Z, Y), dma(2, Z, Y),
        ],
        compiler_params=pltpu.CompilerParams(collective_id=0, has_side_effects=True, vmem_limit_bytes=28 << 20),
        cost_estimate=pl.CostEstimate(flops=1 << 31, bytes_accessed=8 << 20, transcendentals=0),
    )(*(pltpu.with_memory_space_constraint(x, pltpu.HBM) for x in (mom, grad, q_in, weight)))
    weight_new, momentum_new, q_new = pl.pallas_call(
        finish,
        out_shape=(
            jax.ShapeDtypeStruct((512, 2048), F32),
            jax.ShapeDtypeStruct((512, 2048), F32),
            jax.ShapeDtypeStruct((2048, 128), F32),
        ),
        in_specs=[pl.BlockSpec(memory_space=pltpu.VMEM)] * 5,
        out_specs=(any_, any_, any_),
        scratch_shapes=[vm(512, 2048), vm(512, 2048), vm(2048, 128), dma(8), dma(8), dma(8)],
        compiler_params=pltpu.CompilerParams(vmem_limit_bytes=24 << 20),
        cost_estimate=pl.CostEstimate(flops=1 << 31, bytes_accessed=21 << 20, transcendentals=0),
    )(buffer, weight, right, basis, sq)
    return (weight_new, momentum_new[None], q_new)


def solution(mesh):
    placed = (P("fsdp", "tp"), P("rep", "fsdp", "tp"), P("rep", "fsdp", "tp"), P("tp", None))
    return jax.shard_map(
        shards,
        mesh=mesh,
        in_specs=placed,
        out_specs=(P("fsdp", "tp"), P("rep", "fsdp", "tp"), P("tp", None)),
        check_vma=False,
    )
```

```python
import jax
import jax.numpy as jnp
from jax import lax
from jax.experimental import pallas as pl
from jax.experimental.pallas import tpu as pltpu
from jax.sharding import PartitionSpec as P

MESH = pl.DeviceIdType.MESH
F32 = jnp.float32
BF16 = jnp.bfloat16
Z, T, Y = 8, 8, 4
G = T * Y


def split(x):
    hi = x.astype(BF16)
    return hi, (x - hi.astype(F32)).astype(BF16)


def mm(a, b, dims=((1,), (0,))):
    return lax.dot_general(a, b, (dims, ((), ())), preferred_element_type=F32)


def mmf(a, b, dims=((1,), (0,))):
    return lax.dot_general(a, b, (dims, ((), ())), precision=lax.Precision.HIGHEST, preferred_element_type=F32)


class Exchange:
    def __init__(self, n, me, device, src, dst, send, recv):
        self.n, self.me, self.device, self.src, self.dst = n, me, device, src, dst
        self.send, self.recv = send, recv

    def each(self, body):
        order = {Z: (4, 3, 5, 2, 6, 1, 7), Y: (2, 1, 3)}.get(self.n, range(1, self.n))
        for o in order:
            body(lax.rem(self.me + o, self.n))

    def copy(self, j, slot):
        return pltpu.make_async_remote_copy(
            src_ref=self.src(j),
            dst_ref=self.dst(slot),
            send_sem=self.send.at[j],
            recv_sem=self.recv.at[slot],
            device_id=self.device(j),
            device_id_type=MESH,
        )

    def start_one(self, j):
        self.copy(j, self.me).start()

    def recv_one(self, j):
        self.copy(j, j).wait_recv()

    def start(self):
        self.each(lambda j: self.copy(j, self.me).start())

    def wait_recv(self):
        self.each(lambda j: self.copy(j, j).wait_recv())

    def wait_send(self):
        self.each(lambda j: self.copy(j, self.me).wait_send())


def total(ref, n):
    acc = ref[0]
    for k in range(1, n):
        acc = acc + ref[k]
    return acc


def factor(work, gram):
    rows = lax.broadcasted_iota(jnp.int32, (128, 128), 0)
    lanes = lax.broadcasted_iota(jnp.int32, (128, 128), 1)
    lane = lanes[0:1]
    work[:, 0:128] = gram
    work[:, 128:256] = jnp.where(rows == lanes, 1.0, 0.0).astype(F32)
    for low in range(0, 128, 32):
        below = lax.broadcasted_iota(jnp.int32, (128 - low, 1), 0) + low
        wide = lanes[low:128]

        def step(k, carry):
            j = 4 * k
            row = [work[pl.ds(j + s, 1), :] for s in range(4)]
            left = work[low:128, 0:128]
            col = [jnp.sum(jnp.where(wide == j + s, left, 0.0), axis=1, keepdims=True) for s in range(4)]
            e = {}
            for a in range(4):
                for b in range(a, 4):
                    e[a, b] = jnp.sum(jnp.where(lane == j + b, row[a][:, 0:128], 0.0), axis=1, keepdims=True)
            update = None
            for a in range(4):
                inv = 1.0 / e[a, a]
                for b in range(a + 1, 4):
                    q = e[a, b] * inv
                    row[b] = row[b] - q * row[a]
                    for c in range(b, 4):
                        e[b, c] = e[b, c] - q * e[a, c]
                    col[b] = col[b] - q * col[a]
                term = jnp.where(below > j + 3, col[a] * inv, 0.0) * row[a]
                update = term if update is None else update + term
            work[low:128, :] = work[low:128, :] - update
            for a in range(1, 4):
                work[pl.ds(j + a, 1), :] = row[a]
            return carry

        lax.fori_loop(low // 4, low // 4 + 8, step, 0)
        yield


def inverse_factor(work):
    rows = lax.broadcasted_iota(jnp.int32, (128, 128), 0)
    lanes = lax.broadcasted_iota(jnp.int32, (128, 128), 1)
    d = jnp.sum(jnp.where(rows == lanes, work[:, 0:128], 0.0), axis=1, keepdims=True)
    return work[:, 128:256] * lax.rsqrt(d)


def talk(
    mom, grad, q_in, weight, right_out, basis_out, sq_out, buffer_out, weight_out,
    mom_v, grad_v, q_v, hi_v, lo_v, q_hl,
    part, part_r, proj, gram_p, gram_r, gram,
    wa, wb, ra1, rb1, sa1, sb1, ra2, rb2, rta, rtb,
    work, basis_v, sq_p, sq_z,
    load, store, s_tp, r_tp, s_z, r_z, s_y, r_y, s_pa, r_pa, s_pb, r_pb,
):
    f, t, r = lax.axis_index("fsdp"), lax.axis_index("tp"), lax.axis_index("rep")
    g = t * Y + r

    loads = [pltpu.make_async_copy(q_in, q_v, load.at[8])]
    for c in range(4):
        cols = pl.ds(512 * c, 512)
        loads.append(pltpu.make_async_copy(mom.at[:, cols], mom_v.at[:, cols], load.at[2 * c]))
        loads.append(pltpu.make_async_copy(grad.at[:, cols], grad_v.at[:, cols], load.at[2 * c + 1]))
    for cp in loads:
        cp.start()
    keep_weight = pltpu.make_async_copy(weight, weight_out, load.at[9])

    plane = lambda j: {"tp": lax.div(j, Y), "rep": lax.rem(j, Y)}
    along_z = lambda j: {"fsdp": j}
    along_y = lambda j: {"rep": j}

    barrier = pltpu.get_barrier_semaphore()

    def greet(n, me, device):
        def step(o, carry):
            pl.semaphore_signal(barrier, inc=1, device_id=device(lax.rem(me + o, n)), device_id_type=MESH)
            return carry

        lax.fori_loop(1, n, step, 0)

    greet(G, g, plane)
    greet(Z, f, along_z)

    ex_part = Exchange(G, g, plane, lambda j: part.at[j], lambda i: part_r.at[i], s_tp.at[0], r_tp.at[0])
    ex_proj = Exchange(G, g, plane, lambda j: proj.at[g], lambda i: proj.at[i], s_tp.at[1], r_tp.at[1])
    ex_gram = Exchange(Z, f, along_z, lambda j: gram_p.at[j], lambda i: gram_r.at[i], s_z.at[0], r_z.at[0])
    ex_gall = Exchange(Z, f, along_z, lambda j: gram.at[f], lambda i: gram.at[i], s_z.at[1], r_z.at[1])
    ex_a2 = Exchange(Y, r, along_y, lambda j: sa1.at[j], lambda i: ra2.at[i], s_y.at[0], r_y.at[0])
    ex_b2 = Exchange(Z, f, along_z, lambda j: sb1.at[j], lambda i: rb2.at[i], s_z.at[2], r_z.at[2])

    def ex_a1(p):
        return Exchange(Z, f, along_z, lambda j: wa.at[j, p], lambda i: ra1.at[i, p], s_pa.at[0, p], r_pa.at[0, p])

    def ex_b1(p):
        return Exchange(Y, r, along_y, lambda j: wb.at[j, p], lambda i: rb1.at[i, p], s_pb.at[0, p], r_pb.at[0, p])

    ga1 = Exchange(Y, r, along_y, lambda j: rta.at[f, r], lambda i: rta.at[f, i], s_y.at[1], r_y.at[1])
    gb1 = Exchange(Z, f, along_z, lambda j: rtb.at[r, f], lambda i: rtb.at[r, i], s_z.at[3], r_z.at[3])

    def ga2(p):
        return Exchange(Z, f, along_z, lambda j: rta.at[f, p], lambda i: rta.at[i, p], s_pa.at[1, p], r_pa.at[1, p])

    def gb2(p):
        return Exchange(Y, r, along_y, lambda j: rtb.at[r, p], lambda i: rtb.at[i, p], s_pb.at[1, p], r_pb.at[1, p])

    ex_qp = Exchange(G, g, plane, lambda j: sq_p.at[g], lambda i: sq_p.at[i], s_tp.at[2], r_tp.at[2])
    ex_qz = Exchange(Z, f, along_z, lambda j: sq_z.at[f], lambda i: sq_z.at[i], s_z.at[4], r_z.at[4])

    loads[0].wait()
    q_h, q_l = split(q_v[...])
    q_hl[:, 0:128] = q_h
    q_hl[:, 128:256] = q_l
    acc = None
    for c in range(4):
        cols = pl.ds(512 * c, 512)
        loads[2 * c + 1].wait()
        loads[2 * c + 2].wait()
        b = mom_v[:, cols] + grad_v[:, cols].astype(F32)
        mom_v[:, cols] = b
        b_h, b_l = split(b)
        hi_v[:, cols] = b_h
        lo_v[:, cols] = b_l
        both = mm(b_h, q_hl[cols, :])
        term = both[:, 0:128] + (both[:, 128:256] + mm(b_l, q_hl[cols, 0:128]))
        acc = term if acc is None else acc + term
    part[...] = acc.reshape(G, 16, 128)
    part_r[pl.ds(g, 1)] = part[pl.ds(g, 1)]

    pl.semaphore_wait(barrier, G + Z - 2)
    keep_weight.start()
    keep_buffer = pltpu.make_async_copy(mom_v, buffer_out, load.at[10])
    keep_buffer.start()
    ex_part.start()
    ex_part.wait_recv()
    proj[pl.ds(g, 1)] = total(part_r, G)[None]
    ex_proj.start()
    ex_proj.wait_recv()

    p_all = proj[...].reshape(512, 128)
    pt = p_all.T
    pt_h, pt_l = split(pt)
    gram_p[...] = mmf(pt, p_all).reshape(Z, 16, 128)
    gram_r[pl.ds(f, 1)] = gram_p[pl.ds(f, 1)]
    ex_gram.start()

    def columns(lo, n):
        b_h = hi_v[:, lo : lo + n]
        w = mm(pt_h, b_h) + (mm(pt_l, b_h) + mm(pt_h, lo_v[:, lo : lo + n]))
        return w.T

    order_a = [lax.rem(r + o, Y) for o in (2, 1, 3, 0)]
    order_b = [lax.rem(f + o, Z) for o in (4, 3, 5, 2, 6, 1, 7, 0)]

    def take_a(p, last=False):
        ex_a1(p).wait_recv()
        acc = wa[f, p]
        for o in range(1, Z):
            acc = acc + ra1[lax.rem(f + o, Z), p]
        if last:
            return acc
        sa1[p] = acc
        ex_a2.start_one(p)

    def take_b(p, last=False):
        ex_b1(p).wait_recv()
        acc = wb[r, p]
        for o in range(1, Y):
            acc = acc + rb1[lax.rem(r + o, Y), p]
        if last:
            return acc
        sb1[p] = acc
        ex_b2.start_one(p)

    wa[...] = columns(0, 512).reshape(Z, Y, 16, 128)
    for p in order_a[0:2]:
        ex_a1(p).start()
    for c in range(2):
        wb[2 * c : 2 * c + 2] = columns(512 + 768 * c, 768).reshape(2, Z, 48, 128)
    for p in order_b:
        ex_b1(p).start()
    ex_gram.wait_recv()
    gram[pl.ds(f, 1)] = total(gram_r, Z)[None]
    ex_gall.start()
    for p in order_a[2:4]:
        ex_a1(p).start()

    for p in order_b[0:2]:
        take_b(p)
    take_a(order_a[0])
    take_b(order_b[2])
    ex_gall.wait_recv()
    steps = factor(work, gram[...].reshape(128, 128))
    next(steps)
    take_b(order_b[3])
    take_b(order_b[4])
    take_a(order_a[1])
    next(steps)
    take_b(order_b[5])
    take_a(order_a[2])
    next(steps)
    take_b(order_b[6])
    own_a = take_a(order_a[3], last=True)
    next(steps)
    own_b = take_b(order_b[7], last=True)
    inverse = inverse_factor(work)

    ex_a2.wait_recv()
    for o in range(1, Y):
        own_a = own_a + ra2[lax.rem(r + o, Y)]
    ex_b2.wait_recv()
    for o in range(1, Z):
        own_b = own_b + rb2[lax.rem(f + o, Z)]
    w = jnp.concatenate([own_a, own_b], axis=0)
    right = 0.25 * mmf(w, inverse, ((1,), (1,)))
    rta[f, r] = right[0:16]
    rtb[r, f] = right[16:64]
    gb1.start()
    ga1.start()
    squares = jnp.sum(right * right, axis=0, keepdims=True)
    sq_p[g] = jnp.broadcast_to(squares, (8, 128))
    ex_qp.start()
    gb2(f).start()
    ga2(r).start()

    def forward_b(o):
        p = lax.rem(f + o, Z)
        gb1.recv_one(p)
        gb2(p).start()

    def forward_a(o):
        p = lax.rem(r + o, Y)
        ga1.recv_one(p)
        ga2(p).start()

    for o in (1, 7):
        forward_b(o)
    forward_a(1)
    forward_a(3)
    forward_a(2)
    forward_b(2)
    forward_b(6)
    for o in (3, 5, 4):
        forward_b(o)
    ex_qp.wait_recv()
    sq_z[f] = total(sq_p, G)
    ex_qz.start()
    basis_v[...] = mmf(proj[...].reshape(512, 128), inverse, ((1,), (1,)))
    keep_basis = pltpu.make_async_copy(basis_v, basis_out, store.at[0])
    keep_basis.start()
    for o in range(Z):
        gb2(lax.rem(f + o, Z)).wait_recv()
    keep_b = pltpu.make_async_copy(rtb.reshape(1536, 128), right_out.at[512:2048], store.at[1])
    keep_b.start()
    for o in range(Y):
        ga2(lax.rem(r + o, Y)).wait_recv()
    keep_a = pltpu.make_async_copy(rta.reshape(512, 128), right_out.at[0:512], store.at[2])
    keep_a.start()
    ex_qz.wait_recv()
    sq_out[...] = total(sq_z, Z)
    for ex in (ex_part, ex_proj, ex_gram, ex_gall, ex_a2, ex_b2, ga1, gb1, ex_qp, ex_qz):
        ex.wait_send()

    def sent_a(p, carry):
        ex_a1(p).wait_send()
        ga2(p).wait_send()
        return carry

    def sent_b(p, carry):
        ex_b1(p).wait_send()
        gb2(p).wait_send()
        return carry

    lax.fori_loop(0, Y, sent_a, 0)
    lax.fori_loop(0, Z, sent_b, 0)
    keep_weight.wait()
    keep_buffer.wait()
    keep_basis.wait()
    keep_b.wait()
    keep_a.wait()


def finish(buffer, weight, right, basis, sq, weight_out, mom_out, q_out, w_v, m_v, q_v, sem_w, sem_m, sem_q):
    scale = lax.rsqrt(sq[0:1] * (1.0 / 16384.0) + 1e-06)
    nt = ((1,), (1,))
    b = basis[...]
    b_h, b_l = split(b)
    s_h, s_l = split(b * scale)
    copies = []
    for c in range(8):
        cols = pl.ds(256 * c, 256)
        r = right[cols, :]
        r_h, r_l = split(r)
        feedback = mm(b_h, r_h, nt) + (mm(b_h, r_l, nt) + mm(b_l, r_h, nt))
        m_v[:, cols] = buffer[:, cols] - 0.05 * feedback
        copies.append(pltpu.make_async_copy(m_v.at[:, cols], mom_out.at[:, cols], sem_m.at[c]))
        copies[-1].start()
        update = mm(s_h, r_h, nt) + (mm(s_h, r_l, nt) + mm(s_l, r_h, nt))
        w_v[:, cols] = 0.999 * weight[:, cols] - 0.2 * update
        copies.append(pltpu.make_async_copy(w_v.at[:, cols], weight_out.at[:, cols], sem_w.at[c]))
        copies[-1].start()
        q_v[cols, :] = r * scale
        copies.append(pltpu.make_async_copy(q_v.at[cols, :], q_out.at[cols, :], sem_q.at[c]))
        copies[-1].start()
    for cp in copies:
        cp.wait()


def shards(weight, momentum, gradient, q_in):
    mom, grad = momentum[0], gradient[0]
    vm = lambda *shape: pltpu.VMEM(shape, F32)
    dma = lambda *shape: pltpu.SemaphoreType.DMA(shape)
    any_ = pl.BlockSpec(memory_space=pl.ANY)
    hbm = pl.BlockSpec(memory_space=pltpu.HBM)
    right, basis, sq, buffer, weight = pl.pallas_call(
        talk,
        out_shape=(
            jax.ShapeDtypeStruct((2048, 128), F32),
            jax.ShapeDtypeStruct((512, 128), F32),
            jax.ShapeDtypeStruct((8, 128), F32),
            pltpu.VMEM((512, 2048), F32),
            pltpu.VMEM((512, 2048), F32),
        ),
        in_specs=[hbm] * 4,
        out_specs=(any_, any_, pl.BlockSpec(memory_space=pltpu.VMEM), any_, any_),
        scratch_shapes=[
            vm(512, 2048), pltpu.VMEM((512, 2048), BF16), vm(2048, 128),
            pltpu.VMEM((512, 2048), BF16), pltpu.VMEM((512, 2048), BF16), pltpu.VMEM((2048, 256), BF16),
            vm(G, 16, 128), vm(G, 16, 128), vm(G, 16, 128),
            vm(Z, 16, 128), vm(Z, 16, 128), vm(Z, 16, 128),
            vm(Z, Y, 16, 128), vm(Y, Z, 48, 128), vm(Z, Y, 16, 128), vm(Y, Z, 48, 128),
            vm(Y, 16, 128), vm(Z, 48, 128), vm(Y, 16, 128), vm(Z, 48, 128),
            vm(Z, Y, 16, 128), vm(Y, Z, 48, 128),
            vm(128, 256), vm(512, 128), vm(G, 8, 128), vm(Z, 8, 128),
            dma(11), dma(3), dma(3, G), dma(3, G), dma(5, Z), dma(5, Z), dma(2, Y), dma(2, Y),
            dma(2, Y, Z), dma(2, Y, Z), dma(2, Z, Y), dma(2, Z, Y),
        ],
        compiler_params=pltpu.CompilerParams(collective_id=0, has_side_effects=True, vmem_limit_bytes=28 << 20),
        cost_estimate=pl.CostEstimate(flops=1 << 31, bytes_accessed=8 << 20, transcendentals=0),
    )(*(pltpu.with_memory_space_constraint(x, pltpu.HBM) for x in (mom, grad, q_in, weight)))
    weight_new, momentum_new, q_new = pl.pallas_call(
        finish,
        out_shape=(
            jax.ShapeDtypeStruct((512, 2048), F32),
            jax.ShapeDtypeStruct((512, 2048), F32),
            jax.ShapeDtypeStruct((2048, 128), F32),
        ),
        in_specs=[pl.BlockSpec(memory_space=pltpu.VMEM)] * 5,
        out_specs=(any_, any_, any_),
        scratch_shapes=[vm(512, 2048), vm(512, 2048), vm(2048, 128), dma(8), dma(8), dma(8)],
        compiler_params=pltpu.CompilerParams(vmem_limit_bytes=24 << 20),
        cost_estimate=pl.CostEstimate(flops=1 << 31, bytes_accessed=21 << 20, transcendentals=0),
    )(buffer, weight, right, basis, sq)
    return (weight_new, momentum_new[None], q_new)


def solution(mesh):
    placed = (P("fsdp", "tp"), P("rep", "fsdp", "tp"), P("rep", "fsdp", "tp"), P("tp", None))
    return jax.shard_map(
        shards,
        mesh=mesh,
        in_specs=placed,
        out_specs=(P("fsdp", "tp"), P("rep", "fsdp", "tp"), P("tp", None)),
        check_vma=False,
    )
```
